256 devices in a mesh: row: 8 (over x, core), col: 32 (over z, y).
Axes of the slice: x: 4, y: 4, z: 8, core: 2. Of those that a mesh axis runs over, the one named last changes fastest.
Arguments:
- x_saved: bfloat16 [2048, 6144], P('col', 'row'), may hold values from -1.59375 to 1.59375
- out_grad: bfloat16 [2048, 6144], P('col', 'row'), may hold values from -2 to 2
- hidden_pre: bfloat16 [2048, 24576], P('row', 'col'), may hold values from -6 to 6
- w_in: bfloat16 [6144, 24576], P('row', 'col'), may hold values from -0.078125 to 0.078125
- w_out: bfloat16 [24576, 6144], P('col', 'row'), may hold values from -0.0390625 to 0.0390625
Outputs:
- grad_x: bfloat16 [2048, 6144], P('col', 'row')
- grad_w_in: float32 [6144, 24576], P('row', 'col')
- grad_w_out: float32 [24576, 6144], P('col', 'row')
The draws below stay inside these ranges and needn't reach their ends.
All inputs are finite; a program needn't handle non-finite values.
Results may differ from the reference program's by a relative error of at most 0.0049.
Values may be sent and summed in bfloat16 or wider, within the bound.
No kernel may reach another device: no remote copies, remote signals or barrier semaphores. Data moves between devices by JAX's collectives and lax.ppermute only.
A program may use at most 128 MiB of HBM per device.

```python
import jax
import jax.numpy as jnp

D = 6144
FF = 24576
TOKENS = 2048


def levels(own_key, shape, cuts, smallest, high):
    def one(axis_at, parts):
        steps = jax.random.uniform(jax.random.fold_in(jax.random.fold_in(own_key, 6), axis_at), (parts,), jnp.float32, smallest / len(cuts), high / len(cuts))
        return jnp.repeat(jnp.exp(steps), shape[axis_at] // parts).reshape((-1,) + (1,) * (len(shape) - axis_at - 1))

    gain = one(*cuts[0])
    for cut in cuts[1:]:
        gain = gain * one(*cut)
    return gain


def noise(key, extent, scale, bound, split=(), dtype=jnp.bfloat16):
    gain = levels(key, extent, split, -0.22, 0.18) if split else 1.0
    values = jax.random.normal(key, extent, jnp.float32) * scale * gain
    return jnp.minimum(jnp.maximum(values, -bound), bound).astype(dtype)


def setup_inputs(seed: int = 0) -> dict:
    key_list = jax.random.split(jax.random.key(seed), 6)
    return {
        "x_saved": noise(key_list[0], (TOKENS, D), 0.2, 1.59375, ((0, 32), (1, 8))),
        "out_grad": noise(key_list[1], (TOKENS, D), 0.25, 2.0, ((0, 32), (1, 8))),
        "hidden_pre": noise(key_list[2], (TOKENS, FF), 1.0, 6.0, ((0, 8), (1, 32))),
        "w_in": noise(key_list[3], (D, FF), D ** -0.5, 0.078125, ((0, 8), (1, 32))),
        "w_out": noise(key_list[4], (FF, D), FF ** -0.5, 0.0390625, ((0, 32), (1, 8))),
    }


coef = 0.7978845608
cubic = 0.044715


def gelu_value(h):
    t = jnp.tanh(coef * (h + cubic * h * h * h))
    return 0.5 * h * (1.0 + t)


def gelu_slope(h):
    t = jnp.tanh(coef * (h + cubic * h * h * h))
    return 0.5 * (1.0 + t) + 0.5 * h * (1.0 - t * t) * coef * (1.0 + 3.0 * cubic * h * h)


def reference(x_saved, out_grad, hidden_pre, w_in, w_out):
    pre = hidden_pre.astype(jnp.float32)
    activated = gelu_value(pre).astype(jnp.bfloat16)
    dy_wide = out_grad.astype(jnp.float32)
    act_grad = jnp.dot(dy_wide, w_out.astype(jnp.float32).T)
    pre_grad = (act_grad * gelu_slope(pre)).astype(jnp.bfloat16)
    pre_wide = pre_grad.astype(jnp.float32)
    grad_x = jnp.dot(pre_wide, w_in.astype(jnp.float32).T).astype(jnp.bfloat16)
    grad_w_in = jnp.dot(x_saved.astype(jnp.float32).T, pre_wide)
    grad_w_out = jnp.dot(activated.astype(jnp.float32).T, dy_wide)
    return grad_x, grad_w_in, grad_w_out
```

```python
import jax
import jax.numpy as jnp
from jax import lax
from jax.experimental import pallas as pl
from jax.experimental.pallas import tpu as pltpu
from jax.sharding import Mesh, PartitionSpec as P

coef = 0.7978845608
cubic = 0.044715

NX, NC, NZ, NY = 4, 2, 8, 4
BF = jnp.bfloat16
F32 = jnp.float32
GROUPS = ((0, 1, -1, 2, -2, 3, -3, 4),)


def shift(a, axis, by):
    n = lax.axis_size(axis)
    return lax.ppermute(a, axis, [(i, (i + by) % n) for i in range(n)])


def right_product(left, right):
    return lax.dot_general(left, right, (((1,), (1,)), ((), ())), preferred_element_type=F32)


def token_product(left, right):
    return lax.dot_general(left, right, (((0,), (0,)), ((), ())), preferred_element_type=F32)


def roll(blocks, by):
    n = len(blocks)
    index = jnp.full((), by, jnp.int32)
    return [lax.select_n(index, *[blocks[(k + b) % n] for b in range(n)]) for k in range(n)]


def halves(a, core):
    n = a.shape[0] // 2
    low, high = a[:n], a[n:]
    return jnp.where(core == 0, low, high), jnp.where(core == 0, high, low)


def slab_of(shard, x, core):
    shards = [shard, shift(shard, "y", -1), shift(shard, "y", 2), shift(shard, "y", 1)]
    shards = roll(shards, x)
    pairs = [halves(s, core) for s in shards]
    return jnp.concatenate([p[0] for p in pairs] + [p[1] for p in pairs], axis=0)


def ring_gather(slab):
    out = {0: slab}
    for s in range(1, NZ // 2 + 1):
        if s < NZ // 2:
            out[s] = shift(out[s - 1], "z", -1)
        out[-s if s < NZ // 2 else s] = shift(out[1 - s], "z", 1)
    return out


def gelu_kernel(place, pos, hid_ref, act_ref, slope_ref):
    core, first = pos[0], pos[1]
    for h in range(NC):
        for k in range(NX):
            block = lax.rem(first + k, NY)
            half = core if h == 0 else 1 - core
            start = pl.multiple_of(block * 64 + half * 32, 32)
            v = hid_ref[0, pl.ds(start, 32), :].astype(F32)
            t = jnp.tanh(coef * (v + cubic * v * v * v))
            act_ref[0, pl.ds((h * NX + k) * 32, 32), :] = (0.5 * v * (1.0 + t)).astype(BF)
            if h == 0 and k == 0:
                slope = 0.5 * (1.0 + t) + 0.5 * v * (1.0 - t * t) * coef * (1.0 + 3.0 * cubic * v * v)
                slope_ref[0] = slope


def gelu_parts(hidden, place, pos):
    n, rows, cols = hidden.shape
    return pl.pallas_call(
        gelu_kernel,
        grid_spec=pltpu.PrefetchScalarGridSpec(
            num_scalar_prefetch=2,
            grid=(n,),
            in_specs=[pl.BlockSpec((1, rows, cols), lambda s, place, pos: (place[s], 0, 0))],
            out_specs=[
                pl.BlockSpec((1, rows, cols), lambda s, place, pos: (s, 0, 0)),
                pl.BlockSpec((1, rows // 8, cols), lambda s, place, pos: (s, 0, 0)),
            ],
        ),
        out_shape=[
            jax.ShapeDtypeStruct((n, rows, cols), BF),
            jax.ShapeDtypeStruct((n, rows // 8, cols), F32),
        ],
        cost_estimate=pl.CostEstimate(
            flops=20 * n * rows * cols, bytes_accessed=5 * n * rows * cols, transcendentals=n * rows * cols
        ),
        name="gelu_parts",
    )(place, pos, hidden)


ORDER = (0, -1, 1, -2, 2, -3, 3, 4)


def local(x_saved, out_grad, hidden_pre, w_in, w_out):
    x, core, z, y = (lax.axis_index(a).astype(jnp.int32) for a in ("x", "core", "z", "y"))
    width = x_saved.shape[1]
    cotan = ring_gather(slab_of(out_grad, x, core))
    mine = jnp.stack(
        [hidden_pre, shift(hidden_pre, "x", -1), shift(hidden_pre, "x", 2), shift(hidden_pre, "x", 1)]
    )
    hidden = jnp.concatenate([mine, shift(mine, "core", 1)], axis=0)
    owner = jnp.stack([(z + s) % NZ for s in ORDER])
    place = ((owner % NC) ^ core) * NX + (owner // NC - x) % NX
    act, slope = gelu_parts(hidden, place.astype(jnp.int32), jnp.stack([core, (x + y) % NY]))

    pre = {}
    for group in GROUPS:
        q = len(group)
        part = [right_product(cotan[s], w_out).reshape(NC, NX, 32, -1) for s in group]
        keep = jnp.stack([p[0] for p in part], axis=1)
        give = jnp.stack([p[1] for p in part], axis=1).astype(BF)
        both = keep + shift(give, "core", 1).astype(F32)
        sent = both.astype(BF)
        total = both[0]
        for k in range(1, NX):
            total = total + shift(sent[k], "x", k).astype(F32)
        slopes = jnp.stack([slope[ORDER.index(s)] for s in group])
        own = (total * slopes).astype(BF)
        ours = jnp.stack([own, shift(own, "x", -1), shift(own, "x", 2), shift(own, "x", 1)])
        other = shift(ours, "core", 1)
        for i, s in enumerate(group):
            pre[s] = jnp.concatenate([ours[:, i].reshape(128, -1), other[:, i].reshape(128, -1)])

    def term(s):
        return right_product(pre[s], w_in)

    up = term(4)
    down = term(-3)
    for s in (3, 2, 1, 0):
        up = shift(up.astype(BF), "z", 1).astype(F32)
        if s:
            up = up + term(s)
        if s < 3:
            down = shift(down.astype(BF), "z", -1).astype(F32)
            if s:
                down = down + term(-s)
    summed = (term(0) + up + down).reshape(NC, NX, 32, width)
    blocks = roll([summed[:, k] for k in range(NX)], (NX - x) % NX)
    grad_x = blocks[0]
    for j in range(1, NY):
        grad_x = grad_x + shift(blocks[j], "y", j)
    grad_x = jnp.concatenate(halves(grad_x.reshape(64, width), core)).astype(BF)

    inputs = ring_gather(slab_of(lax.optimization_barrier((x_saved, cotan[4]))[0], x, core))
    pre_all = jnp.concatenate([pre[s] for s in ORDER])
    grad_w_in = token_product(jnp.concatenate([inputs[s] for s in ORDER]), pre_all)
    grad_w_out = token_product(
        act.reshape(pre_all.shape), jnp.concatenate([cotan[s] for s in ORDER])
    )
    return (grad_x, grad_w_in, grad_w_out)


def solution(mesh):
    grid = Mesh(mesh.devices.reshape(NX, NC, NZ, NY), ("x", "core", "z", "y"))
    row, col = ("x", "core"), ("z", "y")
    return jax.shard_map(
        local,
        mesh=grid,
        in_specs=(P(col, row), P(col, row), P(row, col), P(row, col), P(col, row)),
        out_specs=(P(col, row), P(row, col), P(col, row)),
        check_vma=False,
    )
```

```python
import functools

import jax
import jax.numpy as jnp
from jax import lax
from jax.experimental import pallas as pl
from jax.experimental.pallas import tpu as pltpu
from jax.sharding import Mesh, PartitionSpec as P

coef = 0.7978845608
cubic = 0.044715

NX, NC, NZ, NY = 4, 2, 8, 4
ROWS, HALF, SHARD = 256, 32, 64
BF = jnp.bfloat16
F32 = jnp.float32
GROUPS = ((0, 1, -1, 2, -2), (3, -3, 4))
ORDER = tuple(s for group in GROUPS for s in group)
BACK = ((4, -3, 3, -2), (2, -1, 1, 0))
FEATURES = 768
LIMIT = 48 * 1024 * 1024


def shift(a, axis, by):
    n = lax.axis_size(axis)
    return lax.ppermute(a, axis, [(i, (i + by) % n) for i in range(n)])


def token_product(left, right):
    return lax.dot_general(left, right, (((0,), (0,)), ((), ())), preferred_element_type=F32)


def right_product(left, right):
    return lax.dot_general(left, right, (((1,), (1,)), ((), ())), preferred_element_type=F32)


def call(body, pos, args, outs, name, flops=0, scratch=(), space=pltpu.VMEM):
    return pl.pallas_call(
        body,
        in_specs=[pl.BlockSpec(memory_space=pltpu.SMEM)]
        + [pl.BlockSpec(memory_space=None if a.shape[0] == FEATURES else space) for a in args],
        out_specs=[pl.BlockSpec(memory_space=pltpu.VMEM)] * len(outs),
        out_shape=outs,
        scratch_shapes=list(scratch),
        compiler_params=pltpu.CompilerParams(vmem_limit_bytes=LIMIT),
        cost_estimate=pl.CostEstimate(flops=1, bytes_accessed=1, transcendentals=0),
        name=name,
    )(pos, *args)


def shape(dtype, *dims):
    return jax.ShapeDtypeStruct(dims, dtype)


def tokens_at(block, half):
    return pl.ds(pl.multiple_of(block * SHARD + half * HALF, HALF), HALF)


def after(a, token):
    if token is None:
        return a
    return lax.optimization_barrier((a, token))[0]


def together(*arrays):
    return list(lax.optimization_barrier(arrays))


def slab_of(shard):
    return jnp.concatenate([shard, shift(shard, "y", -1), shift(shard, "y", 2), shift(shard, "y", 1)])


def slab_start(pos, s, j):
    return lax.rem(pos[3] + (s + NZ), NZ) * ROWS + lax.rem(pos[2] + j, NY) * SHARD


def w_out_kernel(pos, hid_ref, *refs):
    *slabs, out_ref, held = refs
    for i, (s, slab) in enumerate(zip(ORDER, slabs)):
        for j in range(NY):
            start = pl.multiple_of(slab_start(pos, s, j), SHARD)
            v = hid_ref[pl.ds(start, SHARD), :].astype(F32)
            t = jnp.tanh(coef * (v + cubic * v * v * v))
            held[j * SHARD : (j + 1) * SHARD, :] = (0.5 * v * (1.0 + t)).astype(BF)
        term = token_product(held[...], slab[...])
        out_ref[...] = term if i == 0 else out_ref[...] + term


def w_in_kernel(pos, x_ref, *refs):
    *groups, out_ref, held = refs
    for g, group in enumerate(BACK):
        for n, s in enumerate(group):
            for j in range(NY):
                start = pl.multiple_of(slab_start(pos, s, j), SHARD)
                held[j * SHARD : (j + 1) * SHARD, :] = x_ref[pl.ds(start, SHARD), :]
            term = token_product(held[...], groups[g][n])
            out_ref[...] = term if g == n == 0 else out_ref[...] + term


def own_kernel(pos, hid_ref, t0, t1, t2, t3, *out_refs):
    for i, s in enumerate(ORDER):
        start = pl.multiple_of(slab_start(pos, s, pos[0]) + pos[1] * HALF, HALF)
        v = hid_ref[pl.ds(start, HALF), :].astype(F32)
        t = jnp.tanh(coef * (v + cubic * v * v * v))
        slope = 0.5 * (1.0 + t) + 0.5 * v * (1.0 - t * t) * coef * (1.0 + 3.0 * cubic * v * v)
        total = t0[i] + t1[i].astype(F32) + t2[i].astype(F32) + t3[i].astype(F32)
        for group, ref in zip(BACK, out_refs):
            if s in group:
                ref[group.index(s)] = (total * slope).astype(BF)


def act_kernel(q, pos, *refs):
    slabs, (w_ref, keep_ref, give_ref, acc_ref) = refs[:q], refs[q:]
    x, core = pos[0], pos[1]
    for i in range(q):
        acc_ref[...] = right_product(slabs[i][...], w_ref[...])
        for k in range(NX):
            block = lax.rem(x + k, NX)
            keep_ref[k, i] = acc_ref[tokens_at(block, core), :]
            give_ref[k, i] = acc_ref[tokens_at(block, 1 - core), :].astype(BF)


def fold_kernel(n, pos, *refs):
    keeps, gots, (own_ref, *sent_refs) = refs[:n], refs[n : 2 * n], refs[2 * n :]
    first = 0
    for keep_ref, got_ref in zip(keeps, gots):
        slabs = slice(first, first + keep_ref.shape[1])
        first += keep_ref.shape[1]
        own_ref[slabs] = keep_ref[0] + got_ref[0].astype(F32)
        for k in range(1, NX):
            sent_refs[k - 1][slabs] = (keep_ref[k] + got_ref[k].astype(F32)).astype(BF)


def stack_kernel(pos, *refs):
    for k in range(len(refs) - 1):
        refs[-1][k] = refs[k][...]


def out_kernel(pos, ours_ref, other_ref, w_ref, pre_ref, own_ref, s1, s2, s3, acc_ref):
    x, core = pos[0], pos[1]
    for i in range(pre_ref.shape[0]):
        for k in range(NX):
            block = lax.rem(x + k, NX)
            pre_ref[i, tokens_at(block, core), :] = ours_ref[k, i]
            pre_ref[i, tokens_at(block, 1 - core), :] = other_ref[k, i]
        acc_ref[...] = right_product(pre_ref[i], w_ref[...])
        for j, ref in enumerate((own_ref, s1, s2, s3)):
            ref[i] = acc_ref[j * SHARD : (j + 1) * SHARD, :].astype(ref.dtype)


def hop(up, down):
    return [shift(up.astype(BF), "z", 1), shift(down.astype(BF), "z", -1)]


def local(x_saved, out_grad, hidden_pre, w_in, w_out):
    x, core, z, y = (lax.axis_index(a).astype(jnp.int32) for a in ("x", "core", "z", "y"))
    pos = jnp.stack([x, core, y, z])
    width, cols = x_saved.shape[1], hidden_pre.shape[1]
    hidden = lax.all_gather(hidden_pre, ("x", "core"), axis=0, tiled=True)
    flops = 2 * ROWS * width * cols
    cotan = {0: slab_of(out_grad)}

    def ring_step(s):
        cotan[s], cotan[-s] = together(shift(cotan[s - 1], "z", -1), shift(cotan[1 - s], "z", 1))

    def over_x(own):
        return [shift(own, "x", -1), shift(own, "x", 2), shift(own, "x", 1)]

    def stack(own, came):
        (ours,) = call(
            stack_kernel, pos, [own, *came], [shape(BF, NX, own.shape[0], HALF, cols)], "stack_pre"
        )
        return ours

    def back(ours, other):
        q = ours.shape[1]
        return call(
            out_kernel,
            pos,
            [ours, other, w_in],
            [shape(BF, q, ROWS, cols), shape(F32, q, SHARD, width)] + [shape(BF, q, SHARD, width)] * (NY - 1),
            "grad_x_products",
            flops=flops * q,
            scratch=[pltpu.VMEM((ROWS, width), F32)],
        )

    def products(group):
        q = len(group)
        return call(
            functools.partial(act_kernel, q),
            pos,
            [cotan[s] for s in group] + [w_out],
            [shape(F32, NX, q, HALF, cols), shape(BF, NX, q, HALF, cols)],
            "act_products",
            flops=flops * q,
            space=None,
            scratch=[pltpu.VMEM((ROWS, cols), F32)],
        )

    ring_step(1)
    ring_step(2)
    inputs = lax.all_gather(after(x_saved, cotan[2]), ("z", "y"), axis=0, tiled=True)
    keep, give = products(GROUPS[0])
    ring_step(3)
    middle = ROWS // 2
    low, high, give = together(cotan[-3][:middle], cotan[3][middle:], give)
    low, high, got = together(shift(low, "z", 1), shift(high, "z", -1), shift(give, "core", 1))
    cotan[4] = jnp.concatenate([low, high])
    last_keep, give = products(GROUPS[1])
    own, *sent = call(
        functools.partial(fold_kernel, 2),
        pos,
        [keep, last_keep, got, shift(give, "core", 1)],
        [shape(F32, NZ, HALF, cols)] + [shape(BF, NZ, HALF, cols)] * (NX - 1),
        "fold",
    )
    (grad_w_out,) = call(
        w_out_kernel,
        pos,
        [after(hidden, own)] + [cotan[s] for s in ORDER],
        [shape(F32, cols, width)],
        "grad_w_out",
        flops=flops * NZ,
        space=None,
        scratch=[pltpu.VMEM((ROWS, cols), BF)],
    )
    *came, grad_w_out = together(*(shift(a, "x", k + 1) for k, a in enumerate(sent)), grad_w_out)
    own, own_last = call(
        own_kernel, pos, [hidden, own, *came], [shape(BF, len(g), HALF, cols) for g in BACK], "pre_grad"
    )
    *came, own_last = together(*over_x(own), own_last)
    ours = stack(own, came)
    pre, near, *sent = back(ours, shift(ours, "core", 1))
    one, two, three, own_last = together(*sent, own_last)
    *came, one, three, two = together(*over_x(own_last), shift(one, "y", 1), shift(three, "y", 3), two)
    ours = stack(own_last, came)
    ours, two = together(ours, two)
    pre_last, near_last, *last = back(ours, shift(ours, "core", 1))
    near = near + one.astype(F32) + three.astype(F32)
    two, one, three, last_two = together(shift(two, "y", 2), last[0], last[2], last[1])
    near = near + two.astype(F32)
    two = last_two
    b = {s: near[i] for i, s in enumerate(BACK[0])}
    up, down, one, two, three = together(b[4].astype(BF), b[-3].astype(BF), one, two, three)
    up, down, one, three = together(*hop(up, down), shift(one, "y", 1), shift(three, "y", 3))
    up, down = up.astype(F32) + b[3], down.astype(F32) + b[-2]
    up, down, two = together(up.astype(BF), down.astype(BF), two)
    (grad_w_in,) = call(
        w_in_kernel,
        pos,
        [inputs, pre, after(pre_last, up)],
        [shape(F32, width, cols)],
        "grad_w_in",
        flops=flops * NZ,
        space=None,
        scratch=[pltpu.VMEM((ROWS, width), BF)],
    )
    up, down, two, grad_w_in = together(*hop(up, down), shift(two, "y", 2), grad_w_in)
    near = near_last + one.astype(F32) + two.astype(F32) + three.astype(F32)
    b = {s: near[i] for i, s in enumerate(BACK[1])}
    up, down = together((up.astype(F32) + b[2]).astype(BF), (down.astype(F32) + b[-1]).astype(BF))
    up, down = together(*hop(up, down))
    up = shift((up.astype(F32) + b[1]).astype(BF), "z", 1)
    grad_x = (b[0] + up.astype(F32) + down.astype(F32)).astype(BF)
    return (grad_x, grad_w_in, grad_w_out)


def solution(mesh):
    grid = Mesh(mesh.devices.reshape(NX, NC, NZ, NY), ("x", "core", "z", "y"))
    row, col = ("x", "core"), ("z", "y")
    return jax.shard_map(
        local,
        mesh=grid,
        in_specs=(P(col, row), P(col, row), P(row, col), P(row, col), P(col, row)),
        out_specs=(P(col, row), P(row, col), P(col, row)),
        check_vma=False,
    )
```

```python
import functools

import jax
import jax.numpy as jnp
from jax import lax
from jax.experimental import pallas as pl
from jax.experimental.pallas import tpu as pltpu
from jax.sharding import Mesh, PartitionSpec as P

coef = 0.7978845608
cubic = 0.044715

NX, NC, NZ, NY = 4, 2, 8, 4
ROWS, HALF, SHARD = 256, 32, 64
BF = jnp.bfloat16
F32 = jnp.float32
GROUPS = ((0, 1, -1, 2, -2), (3, -3, 4))
ORDER = tuple(s for group in GROUPS for s in group)
BACK = ((3, -3, 2, -2, 4), (-1, 1, 0))
FEATURES = 768
LIMIT = 20 * 1024 * 1024


def shift(a, axis, by):
    n = lax.axis_size(axis)
    return lax.ppermute(a, axis, [(i, (i + by) % n) for i in range(n)])


def token_product(left, right):
    return lax.dot_general(left, right, (((0,), (0,)), ((), ())), preferred_element_type=F32)


def right_product(left, right):
    return lax.dot_general(left, right, (((1,), (1,)), ((), ())), preferred_element_type=F32)


def call(body, pos, args, outs, name, flops=0, scratch=(), space=pltpu.VMEM):
    return pl.pallas_call(
        body,
        in_specs=[pl.BlockSpec(memory_space=pltpu.SMEM)]
        + [pl.BlockSpec(memory_space=None if a.shape[0] == FEATURES else space) for a in args],
        out_specs=[pl.BlockSpec(memory_space=pltpu.VMEM)] * len(outs),
        out_shape=outs,
        scratch_shapes=list(scratch),
        compiler_params=pltpu.CompilerParams(vmem_limit_bytes=LIMIT),
        cost_estimate=pl.CostEstimate(flops=1, bytes_accessed=1, transcendentals=0),
        name=name,
    )(pos, *args)


def shape(dtype, *dims):
    return jax.ShapeDtypeStruct(dims, dtype)


def tokens_at(block, half):
    return pl.ds(pl.multiple_of(block * SHARD + half * HALF, HALF), HALF)


def after(a, token):
    if token is None:
        return a
    return lax.optimization_barrier((a, token))[0]


def together(*arrays):
    return list(lax.optimization_barrier(arrays))


def slab_of(shard):
    return jnp.concatenate([shard, shift(shard, "y", -1), shift(shard, "y", 2), shift(shard, "y", 1)])


def slab_start(pos, s, j):
    return lax.rem(pos[3] + (s + NZ), NZ) * ROWS + lax.rem(pos[2] + j, NY) * SHARD


def w_out_kernel(pos, hid_ref, *refs):
    *slabs, out_ref, held = refs
    for i, (s, slab) in enumerate(zip(ORDER, slabs)):
        for j in range(NY):
            start = pl.multiple_of(slab_start(pos, s, j), SHARD)
            v = hid_ref[pl.ds(start, SHARD), :].astype(F32)
            t = jnp.tanh(coef * (v + cubic * v * v * v))
            held[j * SHARD : (j + 1) * SHARD, :] = (0.5 * v * (1.0 + t)).astype(BF)
        term = token_product(held[...], slab[...])
        out_ref[...] = term if i == 0 else out_ref[...] + term


def w_in_kernel(pos, x_ref, *refs):
    *groups, out_ref, held = refs
    for g, group in enumerate(BACK):
        for n, s in enumerate(group):
            for j in range(NY):
                start = pl.multiple_of(slab_start(pos, s, j), SHARD)
                held[j * SHARD : (j + 1) * SHARD, :] = x_ref[pl.ds(start, SHARD), :]
            term = token_product(held[...], groups[g][n])
            out_ref[...] = term if g == n == 0 else out_ref[...] + term


def own_kernel(pos, hid_ref, t0, t1, t2, t3, *out_refs):
    for i, s in enumerate(ORDER):
        start = pl.multiple_of(slab_start(pos, s, pos[0]) + pos[1] * HALF, HALF)
        v = hid_ref[pl.ds(start, HALF), :].astype(F32)
        t = jnp.tanh(coef * (v + cubic * v * v * v))
        slope = 0.5 * (1.0 + t) + 0.5 * v * (1.0 - t * t) * coef * (1.0 + 3.0 * cubic * v * v)
        total = t0[i] + t1[i].astype(F32) + t2[i].astype(F32) + t3[i].astype(F32)
        for group, ref in zip(BACK, out_refs):
            if s in group:
                ref[group.index(s)] = (total * slope).astype(BF)


def act_kernel(q, pos, *refs):
    slabs, (w_ref, keep_ref, give_ref, acc_ref) = refs[:q], refs[q:]
    x, core = pos[0], pos[1]
    for i in range(q):
        acc_ref[...] = right_product(slabs[i][...], w_ref[...])
        for k in range(NX):
            block = lax.rem(x + k, NX)
            keep_ref[k, i] = acc_ref[tokens_at(block, core), :]
            give_ref[k, i] = acc_ref[tokens_at(block, 1 - core), :].astype(BF)


def fold_kernel(n, pos, *refs):
    keeps, gots, (own_ref, *sent_refs) = refs[:n], refs[n : 2 * n], refs[2 * n :]
    first = 0
    for keep_ref, got_ref in zip(keeps, gots):
        slabs = slice(first, first + keep_ref.shape[1])
        first += keep_ref.shape[1]
        own_ref[slabs] = keep_ref[0] + got_ref[0].astype(F32)
        for k in range(1, NX):
            sent_refs[k - 1][slabs] = (keep_ref[k] + got_ref[k].astype(F32)).astype(BF)


def stack_kernel(pos, *refs):
    for k in range(len(refs) - 1):
        refs[-1][k] = refs[k][...]


def out_kernel(pos, ours_ref, other_ref, w_ref, pre_ref, own_ref, s1, s2, s3, acc_ref):
    x, core = pos[0], pos[1]
    for i in range(pre_ref.shape[0]):
        for k in range(NX):
            block = lax.rem(x + k, NX)
            pre_ref[i, tokens_at(block, core), :] = ours_ref[k, i]
            pre_ref[i, tokens_at(block, 1 - core), :] = other_ref[k, i]
        acc_ref[...] = right_product(pre_ref[i], w_ref[...])
        for j, ref in enumerate((own_ref, s1, s2, s3)):
            ref[i] = acc_ref[j * SHARD : (j + 1) * SHARD, :].astype(ref.dtype)


def total(i, *parts):
    return sum(p[i].astype(F32) for p in parts)


def hop(up, down):
    return [shift(up.astype(BF), "z", 1), shift(down.astype(BF), "z", -1)]


def local(x_saved, out_grad, hidden_pre, w_in, w_out):
    x, core, z, y = (lax.axis_index(a).astype(jnp.int32) for a in ("x", "core", "z", "y"))
    pos = jnp.stack([x, core, y, z])
    width, cols = x_saved.shape[1], hidden_pre.shape[1]
    flops = 2 * ROWS * width * cols
    hidden = lax.all_gather(hidden_pre, ("x", "core"), axis=0, tiled=True)
    cotan = {0: slab_of(out_grad)}

    def ring_step(s):
        cotan[s], cotan[-s] = together(shift(cotan[s - 1], "z", -1), shift(cotan[1 - s], "z", 1))

    def over_x(own):
        return [shift(own, "x", -1), shift(own, "x", 2), shift(own, "x", 1)]

    def stack(own, came):
        (ours,) = call(
            stack_kernel, pos, [own, *came], [shape(BF, NX, own.shape[0], HALF, cols)], "stack_pre"
        )
        return ours

    def back(ours, other):
        q = ours.shape[1]
        return call(
            out_kernel,
            pos,
            [ours, other, w_in],
            [shape(BF, q, ROWS, cols), shape(F32, q, SHARD, width)] + [shape(BF, q, SHARD, width)] * (NY - 1),
            "grad_x_products",
            flops=flops * q,
            scratch=[pltpu.VMEM((ROWS, width), F32)],
        )

    def products(group):
        q = len(group)
        return call(
            functools.partial(act_kernel, q),
            pos,
            [cotan[s] for s in group] + [w_out],
            [shape(F32, NX, q, HALF, cols), shape(BF, NX, q, HALF, cols)],
            "act_products",
            flops=flops * q,
            space=None,
            scratch=[pltpu.VMEM((ROWS, cols), F32)],
        )

    ring_step(1)
    ring_step(2)
    inputs = lax.all_gather(after(x_saved, cotan[2]), ("z", "y"), axis=0, tiled=True)
    keep, give = products(GROUPS[0])
    ring_step(3)
    middle = ROWS // 2
    low, high, give = together(cotan[-3][:middle], cotan[3][middle:], give)
    low, high, got = together(shift(low, "z", 1), shift(high, "z", -1), shift(give, "core", 1))
    cotan[4] = jnp.concatenate([low, high])
    last_keep, give = products(GROUPS[1])
    own, *sent = call(
        functools.partial(fold_kernel, 2),
        pos,
        [keep, last_keep, got, shift(give, "core", 1)],
        [shape(F32, NZ, HALF, cols)] + [shape(BF, NZ, HALF, cols)] * (NX - 1),
        "fold",
    )
    (grad_w_out,) = call(
        w_out_kernel,
        pos,
        [after(hidden, own)] + [cotan[s] for s in ORDER],
        [shape(F32, cols, width)],
        "grad_w_out",
        flops=flops * NZ,
        space=None,
        scratch=[pltpu.VMEM((ROWS, cols), BF)],
    )
    *came, grad_w_out = together(*(shift(a, "x", k + 1) for k, a in enumerate(sent)), grad_w_out)
    own, own_last = call(
        own_kernel, pos, [hidden, own, *came], [shape(BF, len(g), HALF, cols) for g in BACK], "pre_grad"
    )
    *came, own_last = together(*over_x(own), own_last)
    ours = stack(own, came)
    pre, near, *sent = back(ours, shift(ours, "core", 1))
    one, two, three, own_last = together(*sent, own_last)
    *came, one, three, two = together(*over_x(own_last), shift(one, "y", 1), shift(three, "y", 3), two)
    ours = stack(own_last, came)
    ours, two = together(ours, two)
    pre_last, near_last, *last = back(ours, shift(ours, "core", 1))
    two, last_one, last_three, last_two = together(shift(two, "y", 2), last[0], last[2], last[1])
    b = {s: total(i, near, one, two, three) for i, s in enumerate(BACK[0])}
    up, down, far, one, three, two = together(
        b[3].astype(BF), b[-3].astype(BF), b[4].astype(BF), last_one, last_three, last_two
    )
    up, down, far, one, three = together(
        *hop(up, down), shift(far, "z", 4), shift(one, "y", 1), shift(three, "y", 3)
    )
    up, down = up.astype(F32) + b[2], down.astype(F32) + b[-2]
    up, down, two = together(up.astype(BF), down.astype(BF), two)
    (grad_w_in,) = call(
        w_in_kernel,
        pos,
        [inputs, pre, after(pre_last, up)],
        [shape(F32, width, cols)],
        "grad_w_in",
        flops=flops * NZ,
        space=None,
        scratch=[pltpu.VMEM((ROWS, width), BF)],
    )
    up, down, two, grad_w_in = together(*hop(up, down), shift(two, "y", 2), grad_w_in)
    b = {s: total(i, near_last, one, two, three) for i, s in enumerate(BACK[1])}
    up, down = up.astype(F32) + b[1], down.astype(F32) + b[-1]
    up, down = together(*hop(*together(up.astype(BF), down.astype(BF))))
    grad_x = (b[0] + far.astype(F32) + up.astype(F32) + down.astype(F32)).astype(BF)
    return (grad_x, grad_w_in, grad_w_out)


def solution(mesh):
    grid = Mesh(mesh.devices.reshape(NX, NC, NZ, NY), ("x", "core", "z", "y"))
    row, col = ("x", "core"), ("z", "y")
    return jax.shard_map(
        local,
        mesh=grid,
        in_specs=(P(col, row), P(col, row), P(row, col), P(row, col), P(col, row)),
        out_specs=(P(col, row), P(row, col), P(col, row)),
        check_vma=False,
    )
```

```python
import functools

import jax
import jax.numpy as jnp
from jax import lax
from jax.experimental import pallas as pl
from jax.experimental.pallas import tpu as pltpu
from jax.sharding import Mesh, PartitionSpec as P

coef = 0.7978845608
cubic = 0.044715

NX, NC, NZ, NY = 4, 2, 8, 4
ROWS, HALF, SHARD = 256, 32, 64
BF = jnp.bfloat16
F32 = jnp.float32
GROUPS = ((0, 1, -1, 2, -2), (3, -3, 4))
ORDER = tuple(s for group in GROUPS for s in group)
BACK = ((4, -3, 3, -2), (2, -1, 1, 0))
FEATURES = 768
LIMIT = 20 * 1024 * 1024


def shift(a, axis, by):
    n = lax.axis_size(axis)
    return lax.ppermute(a, axis, [(i, (i + by) % n) for i in range(n)])


def token_product(left, right):
    return lax.dot_general(left, right, (((0,), (0,)), ((), ())), preferred_element_type=F32)


def right_product(left, right):
    return lax.dot_general(left, right, (((1,), (1,)), ((), ())), preferred_element_type=F32)


def call(body, pos, args, outs, name, flops=0, scratch=(), space=pltpu.VMEM):
    return pl.pallas_call(
        body,
        in_specs=[pl.BlockSpec(memory_space=pltpu.SMEM)]
        + [pl.BlockSpec(memory_space=None if a.shape[0] == FEATURES else space) for a in args],
        out_specs=[pl.BlockSpec(memory_space=pltpu.VMEM)] * len(outs),
        out_shape=outs,
        scratch_shapes=list(scratch),
        compiler_params=pltpu.CompilerParams(vmem_limit_bytes=LIMIT),
        cost_estimate=pl.CostEstimate(flops=1, bytes_accessed=1, transcendentals=0),
        name=name,
    )(pos, *args)


def shape(dtype, *dims):
    return jax.ShapeDtypeStruct(dims, dtype)


def tokens_at(block, half):
    return pl.ds(pl.multiple_of(block * SHARD + half * HALF, HALF), HALF)


def after(a, token):
    if token is None:
        return a
    return lax.optimization_barrier((a, token))[0]


def together(*arrays):
    return list(lax.optimization_barrier(arrays))


def slab_of(shard):
    return jnp.concatenate([shard, shift(shard, "y", -1), shift(shard, "y", 2), shift(shard, "y", 1)])


def slab_start(pos, s, j):
    return lax.rem(pos[3] + (s + NZ), NZ) * ROWS + lax.rem(pos[2] + j, NY) * SHARD


def w_out_kernel(pos, hid_ref, *refs):
    *slabs, out_ref, held = refs
    for i, (s, slab) in enumerate(zip(ORDER, slabs)):
        for j in range(NY):
            start = pl.multiple_of(slab_start(pos, s, j), SHARD)
            v = hid_ref[pl.ds(start, SHARD), :].astype(F32)
            t = jnp.tanh(coef * (v + cubic * v * v * v))
            held[j * SHARD : (j + 1) * SHARD, :] = (0.5 * v * (1.0 + t)).astype(BF)
        term = token_product(held[...], slab[...])
        out_ref[...] = term if i == 0 else out_ref[...] + term


def w_in_kernel(pos, x_ref, *refs):
    *groups, out_ref, held = refs
    for g, group in enumerate(BACK):
        for n, s in enumerate(group):
            for j in range(NY):
                start = pl.multiple_of(slab_start(pos, s, j), SHARD)
                held[j * SHARD : (j + 1) * SHARD, :] = x_ref[pl.ds(start, SHARD), :]
            term = token_product(held[...], groups[g][n])
            out_ref[...] = term if g == n == 0 else out_ref[...] + term


def own_kernel(pos, hid_ref, t0, t1, t2, t3, *out_refs):
    for i, s in enumerate(ORDER):
        start = pl.multiple_of(slab_start(pos, s, pos[0]) + pos[1] * HALF, HALF)
        v = hid_ref[pl.ds(start, HALF), :].astype(F32)
        t = jnp.tanh(coef * (v + cubic * v * v * v))
        slope = 0.5 * (1.0 + t) + 0.5 * v * (1.0 - t * t) * coef * (1.0 + 3.0 * cubic * v * v)
        total = t0[i] + t1[i].astype(F32) + t2[i].astype(F32) + t3[i].astype(F32)
        for group, ref in zip(BACK, out_refs):
            if s in group:
                ref[group.index(s)] = (total * slope).astype(BF)


def act_kernel(q, pos, *refs):
    slabs, (w_ref, keep_ref, give_ref, acc_ref) = refs[:q], refs[q:]
    x, core = pos[0], pos[1]
    for i in range(q):
        acc_ref[...] = right_product(slabs[i][...], w_ref[...])
        for k in range(NX):
            block = lax.rem(x + k, NX)
            keep_ref[k, i] = acc_ref[tokens_at(block, core), :]
            give_ref[k, i] = acc_ref[tokens_at(block, 1 - core), :].astype(BF)


def fold_kernel(n, pos, *refs):
    keeps, gots, (own_ref, *sent_refs) = refs[:n], refs[n : 2 * n], refs[2 * n :]
    first = 0
    for keep_ref, got_ref in zip(keeps, gots):
        slabs = slice(first, first + keep_ref.shape[1])
        first += keep_ref.shape[1]
        own_ref[slabs] = keep_ref[0] + got_ref[0].astype(F32)
        for k in range(1, NX):
            sent_refs[k - 1][slabs] = (keep_ref[k] + got_ref[k].astype(F32)).astype(BF)


def stack_kernel(pos, *refs):
    for k in range(len(refs) - 1):
        refs[-1][k] = refs[k][...]


def out_kernel(pos, ours_ref, other_ref, w_ref, pre_ref, own_ref, s1, s2, s3, acc_ref):
    x, core = pos[0], pos[1]
    for i in range(pre_ref.shape[0]):
        for k in range(NX):
            block = lax.rem(x + k, NX)
            pre_ref[i, tokens_at(block, core), :] = ours_ref[k, i]
            pre_ref[i, tokens_at(block, 1 - core), :] = other_ref[k, i]
        acc_ref[...] = right_product(pre_ref[i], w_ref[...])
        for j, ref in enumerate((own_ref, s1, s2, s3)):
            ref[i] = acc_ref[j * SHARD : (j + 1) * SHARD, :].astype(ref.dtype)


def hop(up, down):
    return [shift(up.astype(BF), "z", 1), shift(down.astype(BF), "z", -1)]


def local(x_saved, out_grad, hidden_pre, w_in, w_out):
    x, core, z, y = (lax.axis_index(a).astype(jnp.int32) for a in ("x", "core", "z", "y"))
    pos = jnp.stack([x, core, y, z])
    width, cols = x_saved.shape[1], hidden_pre.shape[1]
    hidden = lax.all_gather(hidden_pre, ("x", "core"), axis=0, tiled=True)
    flops = 2 * ROWS * width * cols
    cotan = {0: slab_of(out_grad)}

    def ring_step(s):
        cotan[s], cotan[-s] = together(shift(cotan[s - 1], "z", -1), shift(cotan[1 - s], "z", 1))

    def over_x(own):
        return [shift(own, "x", -1), shift(own, "x", 2), shift(own, "x", 1)]

    def stack(own, came):
        (ours,) = call(
            stack_kernel, pos, [own, *came], [shape(BF, NX, own.shape[0], HALF, cols)], "stack_pre"
        )
        return ours

    def back(ours, other):
        q = ours.shape[1]
        return call(
            out_kernel,
            pos,
            [ours, other, w_in],
            [shape(BF, q, ROWS, cols), shape(F32, q, SHARD, width)] + [shape(BF, q, SHARD, width)] * (NY - 1),
            "grad_x_products",
            flops=flops * q,
            scratch=[pltpu.VMEM((ROWS, width), F32)],
        )

    def products(group):
        q = len(group)
        return call(
            functools.partial(act_kernel, q),
            pos,
            [cotan[s] for s in group] + [w_out],
            [shape(F32, NX, q, HALF, cols), shape(BF, NX, q, HALF, cols)],
            "act_products",
            flops=flops * q,
            space=None,
            scratch=[pltpu.VMEM((ROWS, cols), F32)],
        )

    ring_step(1)
    ring_step(2)
    inputs = lax.all_gather(after(x_saved, cotan[2]), ("z", "y"), axis=0, tiled=True)
    keep, give = products(GROUPS[0])
    ring_step(3)
    middle = ROWS // 2
    low, high, give = together(cotan[-3][:middle], cotan[3][middle:], give)
    low, high, got = together(shift(low, "z", 1), shift(high, "z", -1), shift(give, "core", 1))
    cotan[4] = jnp.concatenate([low, high])
    last_keep, give = products(GROUPS[1])
    own, *sent = call(
        functools.partial(fold_kernel, 2),
        pos,
        [keep, last_keep, got, shift(give, "core", 1)],
        [shape(F32, NZ, HALF, cols)] + [shape(BF, NZ, HALF, cols)] * (NX - 1),
        "fold",
    )
    (grad_w_out,) = call(
        w_out_kernel,
        pos,
        [after(hidden, own)] + [cotan[s] for s in ORDER],
        [shape(F32, cols, width)],
        "grad_w_out",
        flops=flops * NZ,
        space=None,
        scratch=[pltpu.VMEM((ROWS, cols), BF)],
    )
    *came, grad_w_out = together(*(shift(a, "x", k + 1) for k, a in enumerate(sent)), grad_w_out)
    own, own_last = call(
        own_kernel, pos, [hidden, own, *came], [shape(BF, len(g), HALF, cols) for g in BACK], "pre_grad"
    )
    *came, own_last = together(*over_x(own), own_last)
    ours = stack(own, came)
    pre, near, *sent = back(ours, shift(ours, "core", 1))
    one, two, three, own_last = together(*sent, own_last)
    *came, one, three, two = together(*over_x(own_last), shift(one, "y", 1), shift(three, "y", 3), two)
    ours = stack(own_last, came)
    ours, two = together(ours, two)
    pre_last, near_last, *last = back(ours, shift(ours, "core", 1))
    near = near + one.astype(F32) + three.astype(F32)
    two, one, three, last_two = together(shift(two, "y", 2), last[0], last[2], last[1])
    near = near + two.astype(F32)
    two = last_two
    b = {s: near[i] for i, s in enumerate(BACK[0])}
    up, down, one, two, three = together(b[4].astype(BF), b[-3].astype(BF), one, two, three)
    up, down, one, three = together(*hop(up, down), shift(one, "y", 1), shift(three, "y", 3))
    up, down = up.astype(F32) + b[3], down.astype(F32) + b[-2]
    up, down, two = together(up.astype(BF), down.astype(BF), two)
    (grad_w_in,) = call(
        w_in_kernel,
        pos,
        [inputs, pre, after(pre_last, up)],
        [shape(F32, width, cols)],
        "grad_w_in",
        flops=flops * NZ,
        space=None,
        scratch=[pltpu.VMEM((ROWS, width), BF)],
    )
    up, down, two, grad_w_in = together(*hop(up, down), shift(two, "y", 2), grad_w_in)
    near = near_last + one.astype(F32) + two.astype(F32) + three.astype(F32)
    b = {s: near[i] for i, s in enumerate(BACK[1])}
    up, down = together((up.astype(F32) + b[2]).astype(BF), (down.astype(F32) + b[-1]).astype(BF))
    up, down = together(*hop(up, down))
    up = shift((up.astype(F32) + b[1]).astype(BF), "z", 1)
    grad_x = (b[0] + up.astype(F32) + down.astype(F32)).astype(BF)
    return (grad_x, grad_w_in, grad_w_out)


def solution(mesh):
    grid = Mesh(mesh.devices.reshape(NX, NC, NZ, NY), ("x", "core", "z", "y"))
    row, col = ("x", "core"), ("z", "y")
    return jax.shard_map(
        local,
        mesh=grid,
        in_specs=(P(col, row), P(col, row), P(row, col), P(row, col), P(col, row)),
        out_specs=(P(col, row), P(row, col), P(col, row)),
        check_vma=False,
    )
```
